128 devices in a mesh: dap: 16 (over y, z_hi, core), hc: 8 (over x, z_lo).
Axes of the slice: x: 4, y: 4, z: 4 (z_hi: 2, z_lo: 2; z = z_hi * 2 + z_lo), core: 2. Of those that a mesh axis runs over, the one named last changes fastest.
Arguments:
- alignment: bfloat16 [128, 1024, 256], P('dap'), may hold values from -6 to 6
- align_mask: int32 [128, 1024], P('dap'), may hold values 0 or 1
- residue_mask: int32 [1024], replicated, may hold values 0 or 1
- chain_index: int32 [1024], replicated, may hold values from 0 to 7, never falling along the last dimension, each value on 1 to 512 neighbouring positions
- pair_input: bfloat16 [1024, 1024, 128], P('dap', 'hc'), may hold values from -6 to 6
- offset_table: bfloat16 [66, 128], replicated, may hold values from -6 to 6
- bias_weight: bfloat16 [128, 8], replicated, may hold values from -16 to 16
- query_weight: bfloat16 [256, 256], P(None, 'hc'), may hold values from -0.375 to 0.375
- key_weight: bfloat16 [256, 256], P(None, 'hc'), may hold values from -0.375 to 0.375
- value_weight: bfloat16 [256, 256], P(None, 'hc'), may hold values from -0.375 to 0.375
- gate_weight: bfloat16 [256, 256], P(None, 'hc'), may hold values from -0.375 to 0.375
- output_weight: bfloat16 [256, 256], replicated, may hold values from -0.375 to 0.375
- left_gate_weight: bfloat16 [128, 128], replicated, may hold values from -0.5 to 0.5
- left_weight: bfloat16 [128, 128], replicated, may hold values from -0.5 to 0.5
- right_gate_weight: bfloat16 [128, 128], replicated, may hold values from -0.5 to 0.5
- right_weight: bfloat16 [128, 128], replicated, may hold values from -0.5 to 0.5
- update_gate_weight: bfloat16 [128, 128], replicated, may hold values from -0.5 to 0.5
- update_out_weight: bfloat16 [128, 128], replicated, may hold values from -0.5 to 0.5
Outputs:
- alignment_out: bfloat16 [128, 1024, 256], P('dap')
- pair_out: bfloat16 [1024, 1024, 128], P('dap', 'hc')
The draws below stay inside these ranges and needn't reach their ends.
All inputs are finite; a program needn't handle non-finite values. No bound on the sum of `align_mask` on one device may be relied on, other than what follows from the above.
Results may differ from the reference program's by a relative error of at most 0.0079.
Values may be sent and summed in bfloat16 or wider, within the bound.
No kernel may reach another device: no remote copies, remote signals or barrier semaphores. Data moves between devices by JAX's collectives and lax.ppermute only.
A program may use at most 128 MiB of HBM per device.

```python
import math
import jax
import jax.numpy as jnp
import numpy as np
from jax import lax

C_M = 256
C_Z = 128
C_TRI = 128
HEADS = 8
HEAD_DIM = 32
REACH = 32
CHAINS = 8
RESIDUES = 1024
SEQUENCES = 128


def draw_bias_weight(key, part):
    initial = jnp.clip(jax.random.normal(key, (C_Z, HEADS), jnp.float32), -4.0, 4.0) / math.sqrt(C_Z)
    return initial.astype(jnp.bfloat16)


def plant(result, own_key, least, high):
    shape = result.shape
    spot = [jax.random.randint(jax.random.fold_in(own_key, axis), (), 0, shape[axis]) for axis in range(len(shape))]
    result = result.at[tuple(spot)].set(least)
    longest = shape.index(max(shape))
    spot[longest] = (spot[longest] + 1) % shape[longest]
    return result.at[tuple(spot)].set(high)


def block_levels(rng, extent, cuts, smallest, largest):
    loudness, own = 1.0, jax.random.fold_in(rng, 6)
    for dim, blocks in cuts:
        steps = jnp.exp(jax.random.uniform(jax.random.fold_in(own, dim), (blocks,), jnp.float32, smallest / len(cuts), largest / len(cuts)))
        loudness = loudness * jnp.repeat(steps, extent[dim] // blocks).reshape([-1 if axis == dim else 1 for axis in range(len(extent))])
    return loudness


def length_profile(count, total, limit, slope):
    loads = [(1 << 20) // math.isqrt(standing ** slope) + 1 for standing in range(2, count + 1)]
    surplus, given = total - limit - (count - 1), [1] * (count - 1)
    while surplus > 0:
        candidates = [i for i in range(count - 1) if given[i] < limit]
        mass, left = sum([loads[i] for i in candidates]), surplus
        for i in candidates:
            extra = min(limit - given[i], max(1, left * loads[i] // mass), surplus)
            given[i] = given[i] + extra
            surplus = surplus - extra
    return np.array([limit] + given)


def uneven_parts(rng, count, total, limit, lean):
    if count == 2:
        one = jax.random.randint(rng, (), max(1, total - limit), min(limit, total - 1) + 1)
        return jnp.stack([one, total - one])
    tallies = jnp.asarray(length_profile(count, total, limit, lean), jnp.int32)
    twos = (count - 1) // 2
    giver, receiver = tallies[1:1 + 2 * twos:2], tallies[2:2 + 2 * twos:2]
    margin = jnp.minimum(giver - 1, limit - receiver)
    shifted = jax.random.randint(jax.random.fold_in(rng, 1), (twos,), 0, 1 << 20) % (margin + 1)
    tallies = tallies.at[1:1 + 2 * twos:2].set(giver - shifted).at[2:2 + 2 * twos:2].set(receiver + shifted)
    return tallies[jax.random.permutation(jax.random.fold_in(rng, 2), count)]


def gaussian(stream_key, dims, width, limit, cuts=(), held_as=jnp.bfloat16):
    drawn = jax.random.normal(stream_key, dims, jnp.float32) * width
    if len(cuts) > 0:
        drawn = block_levels(stream_key, dims, cuts, -0.22, 0.18) * drawn
    return jnp.clip(drawn, min=-limit, max=limit).astype(held_as)


def setup_inputs(seed: int = 0) -> dict:
    seeds = jax.random.split(jax.random.key(seed), 19)
    alignment = gaussian(seeds[0], (SEQUENCES, RESIDUES, C_M), 1.0, 6.0, ((0, 16),))
    align_mask = plant((jax.random.randint(seeds[1], (SEQUENCES, RESIDUES), 0, 8) < 7).astype(jnp.int32), jax.random.fold_in(seeds[1], 1), 0, 1)
    residue_mask = plant((jax.random.randint(seeds[2], (RESIDUES,), 0, 16) < 15).astype(jnp.int32), jax.random.fold_in(seeds[2], 1), 0, 1)
    chain_index = jnp.searchsorted(jnp.cumsum(uneven_parts(seeds[3], CHAINS, RESIDUES, RESIDUES // 2, 0)), jnp.arange(RESIDUES), side="right").astype(jnp.int32)
    pair_input = gaussian(seeds[4], (RESIDUES, RESIDUES, C_Z), 1.0, 6.0, ((0, 16), (1, 8)))
    offset_table = gaussian(seeds[5], (2 * REACH + 2, C_Z), 1.0, 6.0)
    bias_weight = draw_bias_weight(jax.random.fold_in(seeds[18], 71), 0)
    query_weight = gaussian(seeds[7], (C_M, HEADS * HEAD_DIM), C_M ** -0.5, 0.375, ((1, 8),))
    key_weight = gaussian(seeds[8], (C_M, HEADS * HEAD_DIM), C_M ** -0.5, 0.375, ((1, 8),))
    value_weight = gaussian(seeds[9], (C_M, HEADS * HEAD_DIM), C_M ** -0.5, 0.375, ((1, 8),))
    gate_weight = gaussian(seeds[10], (C_M, HEADS * HEAD_DIM), C_M ** -0.5, 0.375, ((1, 8),))
    output_weight = gaussian(seeds[11], (HEADS * HEAD_DIM, C_M), (HEADS * HEAD_DIM) ** -0.5, 0.375)
    left_gate_weight = gaussian(seeds[12], (C_Z, C_TRI), C_Z ** -0.5, 0.5)
    left_weight = gaussian(seeds[13], (C_Z, C_TRI), C_Z ** -0.5, 0.5)
    right_gate_weight = gaussian(seeds[14], (C_Z, C_TRI), C_Z ** -0.5, 0.5)
    right_weight = gaussian(seeds[15], (C_Z, C_TRI), C_Z ** -0.5, 0.5)
    update_gate_weight = gaussian(seeds[16], (C_Z, C_Z), C_Z ** -0.5, 0.5)
    update_out_weight = gaussian(seeds[17], (C_TRI, C_Z), C_TRI ** -0.5, 0.5)
    return {"alignment": alignment, "align_mask": align_mask, "residue_mask": residue_mask, "chain_index": chain_index, "pair_input": pair_input, "offset_table": offset_table, "bias_weight": bias_weight, "query_weight": query_weight, "key_weight": key_weight, "value_weight": value_weight, "gate_weight": gate_weight, "output_weight": output_weight, "left_gate_weight": left_gate_weight, "left_weight": left_weight, "right_gate_weight": right_gate_weight, "right_weight": right_weight, "update_gate_weight": update_gate_weight, "update_out_weight": update_out_weight}


EPSILON = 1e-05
MASKED = 1000000000.0

def normalize(values, along):
    values = values.astype(jnp.float32)
    average = lax.optimization_barrier(jnp.mean(values, axis=along, keepdims=True))
    centred = values - average
    variance = lax.optimization_barrier(jnp.mean(centred * centred, axis=along, keepdims=True))
    return centred * lax.rsqrt(variance + EPSILON)

def reference(alignment, align_mask, residue_mask, chain_index, pair_input, offset_table, bias_weight, query_weight, key_weight, value_weight, gate_weight, output_weight, left_gate_weight, left_weight, right_gate_weight, right_weight, update_gate_weight, update_out_weight):
    positions = jnp.arange(RESIDUES, dtype=jnp.int32)
    offsets = jnp.clip(positions[:, None] - positions[None, :] + REACH, 0, 2 * REACH)
    bin_index = jnp.where(chain_index[:, None] == chain_index[None, :], offsets, 2 * REACH + 1).astype(jnp.int32)
    pair_state = pair_input.astype(jnp.float32) + offset_table.astype(jnp.float32)[bin_index]
    pair_norm = normalize(pair_state, 2).astype(jnp.bfloat16)
    head_bias = jnp.einsum('ijc,ch->hij', pair_norm.astype(jnp.float32), bias_weight.astype(jnp.float32))
    align_norm = normalize(alignment, 2).astype(jnp.bfloat16)
    key_bias = MASKED * ((align_mask * residue_mask[None, :]).astype(jnp.float32) - 1.0)
    scaling = HEAD_DIM ** (-0.5)

    def per_sequence(members):
        sequence_rows, masking = members
        query_seq = (jnp.dot(sequence_rows, query_weight, preferred_element_type=jnp.float32) * scaling).astype(jnp.bfloat16)
        keys_seq = jnp.dot(sequence_rows, key_weight, preferred_element_type=jnp.float32).astype(jnp.bfloat16)
        values_seq = jnp.dot(sequence_rows, value_weight, preferred_element_type=jnp.float32).astype(jnp.bfloat16)
        gates_seq = jnp.dot(sequence_rows, gate_weight, preferred_element_type=jnp.float32).astype(jnp.bfloat16)
        query_seq = query_seq.reshape(RESIDUES, HEADS, HEAD_DIM).astype(jnp.float32)
        keys_seq = keys_seq.reshape(RESIDUES, HEADS, HEAD_DIM).astype(jnp.float32)
        values_seq = values_seq.reshape(RESIDUES, HEADS, HEAD_DIM).astype(jnp.float32)
        gates_seq = gates_seq.reshape(RESIDUES, HEADS, HEAD_DIM).astype(jnp.float32)
        scores = jnp.einsum('ihd,jhd->hij', query_seq, keys_seq) + head_bias + masking[None, None, :]
        weights = jax.nn.softmax(scores, axis=-1).astype(jnp.bfloat16)
        mixed = jnp.einsum('hij,jhd->ihd', weights.astype(jnp.float32), values_seq)
        mixed = (mixed * jax.nn.sigmoid(gates_seq)).astype(jnp.bfloat16)
        mixed = mixed.reshape(RESIDUES, HEADS * HEAD_DIM)
        return jnp.dot(mixed, output_weight, preferred_element_type=jnp.float32)
    merged = lax.map(per_sequence, (align_norm, key_bias))
    alignment_out = (alignment.astype(jnp.float32) + merged).astype(jnp.bfloat16)
    pair_mask = (residue_mask[:, None] * residue_mask[None, :]).astype(jnp.float32)
    norm_wide = pair_norm.astype(jnp.float32)

    def edge(gate_matrix, proj_matrix):
        gated = jax.nn.sigmoid(jnp.einsum('ikc,ce->eik', norm_wide, gate_matrix.astype(jnp.float32)))
        projected = jnp.einsum('ikc,ce->eik', norm_wide, proj_matrix.astype(jnp.float32))
        return (gated * projected * pair_mask[None, :, :]).astype(jnp.bfloat16)
    left_side = edge(left_gate_weight, left_weight)
    right_side = edge(right_gate_weight, right_weight)

    def per_channel(channel_pair):
        return jnp.dot(channel_pair[0], channel_pair[1].T, preferred_element_type=jnp.float32).astype(jnp.bfloat16)
    triangle = lax.map(per_channel, (left_side, right_side))
    triangle_norm = normalize(triangle, 0).astype(jnp.bfloat16)
    update_gate = jax.nn.sigmoid(jnp.einsum('ijc,ce->ije', norm_wide, update_gate_weight.astype(jnp.float32)))
    update = jnp.einsum('eij,ec->ijc', triangle_norm.astype(jnp.float32), update_out_weight.astype(jnp.float32)) * update_gate
    pair_out = (pair_state + update).astype(jnp.bfloat16)
    return (alignment_out, pair_out)
```

```python
import jax
import jax.numpy as jnp
from jax import lax
from jax.experimental import pallas as pl
from jax.experimental.pallas import tpu as pltpu
from jax.sharding import PartitionSpec as P

HEADS = 8
HEAD_DIM = 32
REACH = 32
EPSILON = 1e-05
MASKED = 1000000000.0
AXES = ("dap", "hc")
BF = jnp.bfloat16
F32 = jnp.float32
VMEM_BYTES = 48 * 1024 * 1024


def params(**more):
    return pltpu.CompilerParams(vmem_limit_bytes=VMEM_BYTES, **more)


def cost(flops, moved, transcendentals=0):
    return pl.CostEstimate(
        flops=flops, bytes_accessed=moved, transcendentals=transcendentals
    )


def place(x, y, z, core):
    dap = (y % 4) * 4 + ((z % 4) // 2) * 2 + core
    return dap * 8 + (x % 4) * 2 + z % 2


def shift(array, move):
    pairs = []
    for x in range(4):
        for y in range(4):
            for z in range(4):
                for core in range(2):
                    pairs.append((place(x, y, z, core), place(*move(x, y, z, core))))
    return lax.ppermute(array, AXES, pairs)


def over_lanes(values):
    average = jnp.mean(values, axis=-1, keepdims=True)
    centred = values - average
    variance = jnp.mean(centred * centred, axis=-1, keepdims=True)
    return centred * lax.rsqrt(variance + EPSILON)


def pair_states(spot, chains_smem, chain_cols, pair_ref, table_ref, rows, first):
    cols = chain_cols.shape[0]
    column = lax.broadcasted_iota(jnp.int32, (cols, 128), 0) + spot[1]
    lane = lax.broadcasted_iota(jnp.int32, (cols, 128), 1)
    parts = []
    for r in range(rows):
        row = spot[0] + first + r
        offset = jnp.clip(row - column + REACH, 0, 2 * REACH)
        slot = jnp.where(chain_cols == chains_smem[row], offset, 2 * REACH + 1)
        parts.append((slot == lane).astype(F32).astype(BF))
    one_hot = jnp.concatenate(parts, axis=0)
    encoded = jnp.dot(one_hot, table_ref[...], preferred_element_type=F32)
    return pair_ref[...].reshape(rows * cols, 128).astype(F32) + encoded


def norm_kernel(
    spot, chains, chain_cols_ref, pair_ref, table_ref, bias_weight_ref, norm_ref, bias_ref, rows
):
    step = pl.program_id(0)
    state = pair_states(
        spot, chains, chain_cols_ref[...], pair_ref, table_ref, rows, step * rows
    )
    normal = over_lanes(state).astype(BF)
    norm_ref[...] = normal.reshape(rows, 128, 128)
    bias = lax.dot_general(
        bias_weight_ref[...], normal, (((1,), (1,)), ((), ())), preferred_element_type=F32
    )
    bias_ref[...] = bias.reshape(HEADS, rows, 128)


def edge_kernel(spot, marks, col_mask_ref, norm_ref, weight_ref, out_ref, rows):
    step = pl.program_id(0)
    normal = norm_ref[...].reshape(rows * 128, 128)
    mask_row = jnp.concatenate(
        [
            col_mask_ref[...] * marks[spot[0] + step * rows + r].astype(F32)
            for r in range(rows)
        ],
        axis=1,
    )
    for side in range(2):
        both = lax.dot_general(
            weight_ref[side * 256 : side * 256 + 256, :],
            normal,
            (((1,), (1,)), ((), ())),
            preferred_element_type=F32,
        )
        edge = jax.nn.sigmoid(both[:128]) * both[128:] * mask_row
        out_ref[:, side] = edge.astype(BF).reshape(128, rows, 128)


def align_kernel(align_ref, weight_ref, out_ref, turned_ref):
    normal = over_lanes(align_ref[0].astype(F32)).astype(BF)
    both = jnp.dot(normal, weight_ref[...], preferred_element_type=F32)
    lane = lax.broadcasted_iota(jnp.int32, both.shape, 1)
    both = jnp.where(lane < HEAD_DIM, both * (HEAD_DIM ** (-0.5)), both)
    out_ref[0] = both.astype(BF)
    turned_ref[0] = both.T.astype(BF)


def attend_kernel(spot, mixed_ref, turned_ref, key_bias_ref, mine_ref, other_ref, out_ref, bias, sems):
    @pl.when(pl.program_id(0) == 0)
    def _():
        half = mine_ref.shape[2]
        own = pl.multiple_of(spot[2] * half, half)
        far = pl.multiple_of((1 - spot[2]) * half, half)
        one = pltpu.make_async_copy(mine_ref, bias.at[:, :, pl.ds(own, half), :], sems.at[0])
        two = pltpu.make_async_copy(other_ref, bias.at[:, :, pl.ds(far, half), :], sems.at[1])
        one.start()
        two.start()
        one.wait()
        two.wait()

    keys = turned_ref[0, HEAD_DIM : 2 * HEAD_DIM, :]
    width = mixed_ref.shape[1]
    lane = lax.broadcasted_iota(jnp.int32, (width, 2 * HEAD_DIM), 1)
    values = mixed_ref[0][:, 2 * HEAD_DIM :]
    values = jnp.where(lane < HEAD_DIM, values, jnp.ones_like(values))
    masking = key_bias_ref[0]
    blocks = 4
    rows = blocks * 64
    for r in range(width // rows):
        here = slice(r * rows, (r + 1) * rows)
        queries = mixed_ref[0, here, :HEAD_DIM]
        scores = jnp.dot(queries, keys, preferred_element_type=F32)
        added = jnp.concatenate(
            [
                bias[r * blocks : (r + 1) * blocks, h].reshape(rows, 128)
                for h in range(HEADS)
            ],
            axis=1,
        )
        scores = scores + added + masking
        top = jnp.max(scores, axis=1, keepdims=True)
        raised = jnp.exp(scores - top).astype(BF)
        total = jnp.dot(raised, values, preferred_element_type=F32).T
        gates = turned_ref[0, 3 * HEAD_DIM :, here].astype(F32)
        result = total[:HEAD_DIM] / total[HEAD_DIM:] * jax.nn.sigmoid(gates)
        out_ref[0, :, here] = result.astype(BF)


def merge_kernel(heads, align_ref, weight_ref, *refs):
    out_ref = refs[-1]
    pieces = refs[: HEADS]
    merged = jnp.concatenate([piece[0] for piece in pieces], axis=0)
    weight = jnp.concatenate(
        [
            weight_ref[pl.ds(pl.multiple_of(heads[p] * HEAD_DIM, HEAD_DIM), HEAD_DIM), :]
            for p in range(HEADS)
        ],
        axis=0,
    )
    update = lax.dot_general(
        merged, weight, (((0,), (0,)), ((), ())), preferred_element_type=F32
    )
    out_ref[0] = (align_ref[0].astype(F32) + update).astype(BF)


def triangle_kernel(left_ref, right_ref, out_ref):
    groups = left_ref.shape[0]
    rows = groups * 64
    residues = right_ref.shape[0] * 64
    total = jnp.zeros((rows, residues), F32)
    for h in range(0, 8, 2):
        left = jnp.concatenate(
            [left_ref[:, h + k, 0].reshape(rows, 128) for k in range(2)], axis=1
        )
        right = jnp.concatenate(
            [right_ref[:, h + k, 0].reshape(residues, 128) for k in range(2)], axis=1
        )
        total = total + lax.dot_general(
            left, right, (((1,), (1,)), ((), ())), preferred_element_type=F32
        )
    for h in range(8):
        out_ref[:, h] = total[:, h * 128 : h * 128 + 128].astype(BF).reshape(groups, 64, 128)


def update_kernel(
    spot, chains, chain_cols_ref, pair_ref, table_ref, norm_ref, triangle_ref, gate_weight_ref,
    out_weight_ref, out_ref, rows
):
    step = pl.program_id(0)
    state = pair_states(
        spot, chains, chain_cols_ref[...], pair_ref, table_ref, rows, step * rows
    )
    gate = jax.nn.sigmoid(
        jnp.dot(
            norm_ref[...].reshape(rows * 128, 128),
            gate_weight_ref[...],
            preferred_element_type=F32,
        )
    )
    values = triangle_ref[...].astype(F32)
    average = jnp.mean(values, axis=0, keepdims=True)
    centred = values - average
    variance = jnp.mean(centred * centred, axis=0, keepdims=True)
    normal = (centred * lax.rsqrt(variance + EPSILON)).reshape(128, rows * 128).astype(BF)
    update = lax.dot_general(
        normal, out_weight_ref[...], (((0,), (0,)), ((), ())), preferred_element_type=F32
    )
    out_ref[...] = (state + update * gate).astype(BF).reshape(rows, 128, 128)


def whole(shape):
    return pl.BlockSpec(shape, lambda *_: (0,) * len(shape))


def norm_call(spot, chains, chain_cols, pair, table, bias_weight, rows=16):
    return pl.pallas_call(
        lambda *refs: norm_kernel(*refs, rows=rows),
        grid_spec=pltpu.PrefetchScalarGridSpec(
            num_scalar_prefetch=2,
            grid=(64 // rows,),
            in_specs=[
                whole((128, 128)),
                pl.BlockSpec((rows, 128, 128), lambda g, *_: (g, 0, 0)),
                whole((128, 128)),
                whole((HEADS, 128)),
            ],
            out_specs=[
                pl.BlockSpec((rows, 128, 128), lambda g, *_: (g, 0, 0)),
                pl.BlockSpec((HEADS, rows, 128), lambda g, *_: (0, g, 0)),
            ],
        ),
        out_shape=[
            jax.ShapeDtypeStruct((64, 128, 128), BF),
            jax.ShapeDtypeStruct((HEADS, 64, 128), F32),
        ],
        compiler_params=params(),
        cost_estimate=cost(600_000_000, 5_000_000),
        name="pair_norm",
    )(spot, chains, chain_cols, pair, table, bias_weight)


def edge_call(spot, marks, col_mask, normal, weights, rows=16):
    return pl.pallas_call(
        lambda *refs: edge_kernel(*refs, rows=rows),
        grid_spec=pltpu.PrefetchScalarGridSpec(
            num_scalar_prefetch=2,
            grid=(64 // rows,),
            in_specs=[
                whole((1, 128)),
                pl.BlockSpec((rows, 128, 128), lambda g, *_: (g, 0, 0)),
                whole((512, 128)),
            ],
            out_specs=pl.BlockSpec((128, 2, rows, 128), lambda g, *_: (0, 0, g, 0)),
        ),
        out_shape=jax.ShapeDtypeStruct((128, 2, 64, 128), BF),
        compiler_params=params(),
        cost_estimate=cost(2_000_000_000, 6_500_000, 2_000_000),
        name="edges",
    )(spot, marks, col_mask, normal, weights)


def align_call(alignment, weights):
    count, residues, width = alignment.shape
    return pl.pallas_call(
        align_kernel,
        grid=(count,),
        in_specs=[
            pl.BlockSpec((1, residues, width), lambda s: (s, 0, 0)),
            whole((width, 128)),
        ],
        out_specs=[
            pl.BlockSpec((1, residues, 128), lambda s: (s, 0, 0)),
            pl.BlockSpec((1, 128, residues), lambda s: (s, 0, 0)),
        ],
        out_shape=[
            jax.ShapeDtypeStruct((count, residues, 128), BF),
            jax.ShapeDtypeStruct((count, 128, residues), BF),
        ],
        compiler_params=params(),
        cost_estimate=cost(540_000_000, 8_400_000),
        name="align_project",
    )(alignment, weights)


def attend_call(spot, mixed, turned, key_bias, mine, other, first, count):
    residues = mixed.shape[1]
    return pl.pallas_call(
        attend_kernel,
        grid_spec=pltpu.PrefetchScalarGridSpec(
            num_scalar_prefetch=1,
            grid=(count,),
            in_specs=[
                pl.BlockSpec((1, residues, 128), lambda s, *_: (s + first, 0, 0)),
                pl.BlockSpec((1, 128, residues), lambda s, *_: (s + first, 0, 0)),
                pl.BlockSpec((1, 1, residues), lambda s, *_: (s + first, 0, 0)),
                pl.BlockSpec(memory_space=pl.ANY),
                pl.BlockSpec(memory_space=pl.ANY),
            ],
            out_specs=pl.BlockSpec((1, HEAD_DIM, residues), lambda s, *_: (s, 0, 0)),
            scratch_shapes=[
                pltpu.VMEM((16, 8, 64, 128), F32),
                pltpu.SemaphoreType.DMA((2,)),
            ],
        ),
        out_shape=jax.ShapeDtypeStruct((count, HEAD_DIM, residues), BF),
        compiler_params=params(),
        cost_estimate=cost(count * 1_500_000_000, 5_000_000, count * 1_000_000),
        name="attend",
    )(spot, mixed, turned, key_bias, mine, other)


def merge_call(heads, alignment, weight, pieces, first, count, before=None):
    _, residues, width = alignment.shape
    extra = [] if before is None else [before]
    return pl.pallas_call(
        merge_kernel,
        grid_spec=pltpu.PrefetchScalarGridSpec(
            num_scalar_prefetch=1,
            grid=(count,),
            in_specs=[
                pl.BlockSpec((1, residues, width), lambda s, *_: (s + first, 0, 0)),
                whole((width, width)),
            ]
            + [pl.BlockSpec((1, HEAD_DIM, residues), lambda s, *_: (s, 0, 0))] * HEADS
            + [pl.BlockSpec(memory_space=pl.ANY)] * len(extra),
            out_specs=pl.BlockSpec((1, residues, width), lambda s, *_: (s + first, 0, 0)),
        ),
        out_shape=jax.ShapeDtypeStruct(alignment.shape, BF),
        input_output_aliases={3 + HEADS: 0} if extra else {},
        compiler_params=params(),
        cost_estimate=cost(count * 140_000_000, count * 1_600_000),
        name="merge_heads",
    )(heads, alignment, weight, *pieces, *extra)


def triangle_call(received, groups=4):
    return pl.pallas_call(
        triangle_kernel,
        grid=(16 // groups,),
        in_specs=[
            pl.BlockSpec((groups, 8, 1, 64, 128), lambda g: (g, 0, 0, 0, 0)),
            pl.BlockSpec((16, 8, 1, 64, 128), lambda g: (0, 0, 1, 0, 0)),
        ],
        out_specs=pl.BlockSpec((groups, 8, 64, 128), lambda g: (g, 0, 0, 0)),
        out_shape=jax.ShapeDtypeStruct((16, 8, 64, 128), BF),
        compiler_params=params(),
        cost_estimate=cost(2_147_483_648, 6_300_000),
        name="triangle",
    )(received, received)


def update_call(spot, chains, chain_cols, pair, table, normal, triangle, gate_w, out_w, rows=16):
    return pl.pallas_call(
        lambda *refs: update_kernel(*refs, rows=rows),
        grid_spec=pltpu.PrefetchScalarGridSpec(
            num_scalar_prefetch=2,
            grid=(64 // rows,),
            in_specs=[
                whole((128, 128)),
                pl.BlockSpec((rows, 128, 128), lambda g, *_: (g, 0, 0)),
                whole((128, 128)),
                pl.BlockSpec((rows, 128, 128), lambda g, *_: (g, 0, 0)),
                pl.BlockSpec((128, rows, 128), lambda g, *_: (0, g, 0)),
                whole((128, 128)),
                whole((128, 128)),
            ],
            out_specs=pl.BlockSpec((rows, 128, 128), lambda g, *_: (g, 0, 0)),
        ),
        out_shape=jax.ShapeDtypeStruct((64, 128, 128), BF),
        compiler_params=params(),
        cost_estimate=cost(900_000_000, 8_400_000, 1_000_000),
        name="pair_update",
    )(spot, chains, chain_cols, pair, table, normal, triangle, gate_w, out_w)


def on_device(
    alignment,
    align_mask,
    residue_mask,
    chain_index,
    pair_input,
    offset_table,
    bias_weight,
    query_weight,
    key_weight,
    value_weight,
    gate_weight,
    output_weight,
    left_gate_weight,
    left_weight,
    right_gate_weight,
    right_weight,
    update_gate_weight,
    update_out_weight,
):
    dap = lax.axis_index("dap")
    hc = lax.axis_index("hc")
    spot = jnp.stack([dap * 64, hc * 128, dap % 2]).astype(jnp.int32)
    chain_part = lax.dynamic_slice_in_dim(chain_index, hc * 128, 128, 0)
    chain_cols = jnp.broadcast_to(chain_part[:, None], (128, 128))
    table = jnp.pad(offset_table, ((0, 128 - offset_table.shape[0]), (0, 0)))
    normal, bias = norm_call(
        spot, chain_index, chain_cols, pair_input, table, bias_weight.T
    )

    halves = bias.reshape(8, 2, 32, 128).transpose(1, 0, 2, 3)
    sent = jnp.broadcast_to(halves[None], (8, 2, 8, 32, 128)).reshape(128, 32, 128)
    mine = lax.all_to_all(sent, AXES, split_axis=0, concat_axis=0, tiled=True)
    other = shift(mine, lambda x, y, z, core: (x, y, z, 1 - core))
    mine = mine.reshape(16, 8, 32, 128)
    other = other.reshape(16, 8, 32, 128)

    col_mask = lax.dynamic_slice_in_dim(residue_mask, hc * 128, 128, 0)
    edge_weights = jnp.concatenate(
        [left_gate_weight.T, left_weight.T, right_gate_weight.T, right_weight.T], axis=0
    )
    edges = edge_call(
        spot, residue_mask, col_mask.astype(F32)[None, :], normal, edge_weights
    )
    qkvg = jnp.concatenate([query_weight, key_weight, value_weight, gate_weight], axis=1)
    mixed, turned = align_call(alignment, qkvg)
    key_bias = MASKED * ((align_mask * residue_mask[None, :]).astype(F32) - 1.0)
    key_bias = key_bias[:, None, :]

    received = lax.all_to_all(edges, AXES, split_axis=0, concat_axis=0, tiled=True)

    one = attend_call(spot, mixed, turned, key_bias, mine, other, 0, 4)
    two = attend_call(spot, mixed, turned, key_bias, mine, other, 4, 4)

    over_z = lambda x, y, z, core: (x, y, z ^ 1, core)
    along = [
        lambda x, y, z, core, d=d: (x + d, y, z, core) for d in (1, 3, 2)
    ]
    ones = [one, shift(one, over_z)]
    ones = ones + [shift(piece, move) for move in along for piece in ones]
    twos = [two] + [shift(two, move) for move in along]
    twos = twos + [shift(piece, over_z) for piece in twos]
    spot_x, spot_z = hc // 2, hc % 2
    order_one = jnp.stack(
        [((spot_x - d) % 4) * 2 + (spot_z ^ f) for d in (0, 1, 3, 2) for f in (0, 1)]
    ).astype(jnp.int32)
    order_two = jnp.stack(
        [((spot_x - d) % 4) * 2 + (spot_z ^ f) for f in (0, 1) for d in (0, 1, 3, 2)]
    ).astype(jnp.int32)
    alignment_out = merge_call(order_one, alignment, output_weight, ones, 0, 4)
    alignment_out = merge_call(
        order_two, alignment, output_weight, twos, 4, 4, alignment_out
    )

    triangle = triangle_call(received.reshape(16, 8, 2, 64, 128))
    back = lax.all_to_all(
        triangle.reshape(128, 64, 128), AXES, split_axis=0, concat_axis=0, tiled=True
    )
    pair_out = update_call(
        spot, chain_index, chain_cols, pair_input, table, normal, back,
        update_gate_weight, update_out_weight
    )
    return (alignment_out, pair_out)


def solution(mesh):
    placed = (
        P("dap", None, None),
        P("dap", None),
        P(),
        P(),
        P("dap", "hc", None),
        P(),
        P(),
        P(None, "hc"),
        P(None, "hc"),
        P(None, "hc"),
        P(None, "hc"),
        P(),
        P(),
        P(),
        P(),
        P(),
        P(),
        P(),
    )
    return jax.shard_map(
        on_device,
        mesh=mesh,
        in_specs=placed,
        out_specs=(P("dap", None, None), P("dap", "hc", None)),
        check_vma=False,
    )
```

```python
import jax
import jax.numpy as jnp
from jax import lax
from jax.experimental import pallas as pl
from jax.experimental.pallas import tpu as pltpu
from jax.sharding import PartitionSpec as P

HEADS = 8
HEAD_DIM = 32
REACH = 32
EPSILON = 1e-05
MASKED = 1000000000.0
AXES = ("dap", "hc")
BF = jnp.bfloat16
F32 = jnp.float32
VMEM_BYTES = 60 * 1024 * 1024


def params(**more):
    return pltpu.CompilerParams(vmem_limit_bytes=VMEM_BYTES, **more)


def cost(flops, moved, transcendentals=0):
    return pl.CostEstimate(
        flops=flops, bytes_accessed=moved, transcendentals=transcendentals
    )


def place(x, y, z, core):
    dap = (y % 4) * 4 + ((z % 4) // 2) * 2 + core
    return dap * 8 + (x % 4) * 2 + z % 2


def shift(array, move):
    pairs = []
    for x in range(4):
        for y in range(4):
            for z in range(4):
                for core in range(2):
                    pairs.append((place(x, y, z, core), place(*move(x, y, z, core))))
    return lax.ppermute(array, AXES, pairs)


def over_lanes(values):
    average = jnp.mean(values, axis=-1, keepdims=True)
    centred = values - average
    variance = jnp.mean(centred * centred, axis=-1, keepdims=True)
    return centred * lax.rsqrt(variance + EPSILON)


def pair_states(spot, chains_smem, chains_ref, pair_ref, table_ref, rows, first):
    cols = 128
    slots = table_ref.shape[0]
    chain_row = chains_ref[pl.ds(spot[1] // cols, 1), :].astype(F32)
    chain_cols = jnp.broadcast_to(chain_row, (cols, cols)).T[:, :slots].astype(jnp.int32)
    column = lax.broadcasted_iota(jnp.int32, (cols, slots), 0) + spot[1]
    lane = lax.broadcasted_iota(jnp.int32, (cols, slots), 1)
    parts = []
    for r in range(rows):
        row = spot[0] + first + r
        offset = jnp.clip(row - column + REACH, 0, 2 * REACH)
        slot = jnp.where(chain_cols == chains_smem[row], offset, 2 * REACH + 1)
        parts.append((slot == lane).astype(F32).astype(BF))
    one_hot = jnp.concatenate(parts, axis=0)
    encoded = jnp.dot(one_hot, table_ref[...], preferred_element_type=F32)
    return pair_ref[...].reshape(rows * cols, 128).astype(F32) + encoded


def norm_kernel(
    spot, chains, chain_rows_ref, pair_ref, table_ref, bias_weight_ref, norm_ref, bias_ref, rows
):
    step = pl.program_id(0)
    state = pair_states(
        spot, chains, chain_rows_ref, pair_ref, table_ref, rows, step * rows
    )
    normal = over_lanes(state).astype(BF)
    norm_ref[...] = normal.reshape(rows, 128, 128)
    bias = lax.dot_general(
        bias_weight_ref[...], normal, (((1,), (1,)), ((), ())), preferred_element_type=F32
    )
    bias_ref[...] = jnp.broadcast_to(bias.reshape(1, 1, HEADS, rows, 128), bias_ref.shape)


def edge_kernel(spot, marks, col_mask_ref, norm_ref, weight_ref, out_ref, rows):
    step = pl.program_id(0)
    normal = norm_ref[...].reshape(rows * 128, 128)
    col_mask = col_mask_ref[pl.ds(spot[1] // 128, 1), :].astype(F32)
    mask_row = jnp.concatenate(
        [
            col_mask * marks[spot[0] + step * rows + r].astype(F32)
            for r in range(rows)
        ],
        axis=1,
    )
    for side in range(2):
        both = lax.dot_general(
            weight_ref[side * 256 : side * 256 + 256, :],
            normal,
            (((1,), (1,)), ((), ())),
            preferred_element_type=F32,
        )
        edge = jax.nn.sigmoid(both[:128]) * both[128:] * mask_row
        out_ref[:, side] = edge.astype(BF).reshape(128, rows, 128)


def align_kernel(align_ref, weight_ref, out_ref, turned_ref):
    normal = over_lanes(align_ref[0].astype(F32)).astype(BF)
    both = jnp.dot(normal, weight_ref[...], preferred_element_type=F32)
    lane = lax.broadcasted_iota(jnp.int32, both.shape, 1)
    both = jnp.where(lane < HEAD_DIM, both * (HEAD_DIM ** (-0.5)), both)
    out_ref[0] = both.astype(BF)
    turned_ref[0] = both.T.astype(BF)


def attend_kernel(spot, mixed_ref, turned_ref, key_bias_ref, mine_ref, other_ref, out_ref, bias, sems):
    @pl.when(pl.program_id(0) == 0)
    def _():
        one = pltpu.make_async_copy(mine_ref, bias.at[:, :, spot[2]], sems.at[0])
        two = pltpu.make_async_copy(other_ref, bias.at[:, :, 1 - spot[2]], sems.at[1])
        one.start()
        two.start()
        one.wait()
        two.wait()

    keys = turned_ref[0, HEAD_DIM : 2 * HEAD_DIM, :]
    width = mixed_ref.shape[1]
    lane = lax.broadcasted_iota(jnp.int32, (width, 2 * HEAD_DIM), 1)
    values = mixed_ref[0][:, 2 * HEAD_DIM :]
    values = jnp.where(lane < HEAD_DIM, values, jnp.ones_like(values))
    masking = key_bias_ref[0]
    blocks = 4
    rows = blocks * 64
    for r in range(width // rows):
        here = slice(r * rows, (r + 1) * rows)
        queries = mixed_ref[0, here, :HEAD_DIM]
        scores = jnp.dot(queries, keys, preferred_element_type=F32)
        added = jnp.concatenate(
            [
                bias[r * blocks : (r + 1) * blocks, h].reshape(rows, 128)
                for h in range(HEADS)
            ],
            axis=1,
        )
        scores = scores + added + masking
        top = jnp.max(scores, axis=1, keepdims=True)
        raised = jnp.exp(scores - top).astype(BF)
        total = jnp.dot(raised, values, preferred_element_type=F32).T
        gates = turned_ref[0, 3 * HEAD_DIM :, here].astype(F32)
        result = total[:HEAD_DIM] / total[HEAD_DIM:] * jax.nn.sigmoid(gates)
        out_ref[0, :, here] = result.astype(BF)


def merge_kernel(heads, align_ref, weight_ref, *refs):
    out_ref = refs[-1]
    pieces = refs[: HEADS]
    merged = jnp.concatenate([piece[0] for piece in pieces], axis=0)
    weight = jnp.concatenate(
        [
            weight_ref[pl.ds(pl.multiple_of(heads[p] * HEAD_DIM, HEAD_DIM), HEAD_DIM), :]
            for p in range(HEADS)
        ],
        axis=0,
    )
    update = lax.dot_general(
        merged, weight, (((0,), (0,)), ((), ())), preferred_element_type=F32
    )
    out_ref[0] = (align_ref[0].astype(F32) + update).astype(BF)


def triangle_kernel(left_ref, right_ref, out_ref):
    groups = left_ref.shape[0]
    rows = groups * 64
    residues = right_ref.shape[0] * 64
    total = jnp.zeros((rows, residues), F32)
    for h in range(0, 8, 2):
        left = jnp.concatenate(
            [left_ref[:, h + k, 0].reshape(rows, 128) for k in range(2)], axis=1
        )
        right = jnp.concatenate(
            [right_ref[:, h + k, 0].reshape(residues, 128) for k in range(2)], axis=1
        )
        total = total + lax.dot_general(
            left, right, (((1,), (1,)), ((), ())), preferred_element_type=F32
        )
    for h in range(8):
        out_ref[:, h] = total[:, h * 128 : h * 128 + 128].astype(BF).reshape(groups, 64, 128)


def update_kernel(
    spot, chains, chain_rows_ref, pair_ref, table_ref, norm_ref, triangle_ref, gate_weight_ref,
    out_weight_ref, out_ref, rows
):
    step = pl.program_id(0)
    state = pair_states(
        spot, chains, chain_rows_ref, pair_ref, table_ref, rows, step * rows
    )
    gate = jax.nn.sigmoid(
        jnp.dot(
            norm_ref[...].reshape(rows * 128, 128),
            gate_weight_ref[...],
            preferred_element_type=F32,
        )
    )
    values = triangle_ref[...].astype(F32)
    average = jnp.mean(values, axis=0, keepdims=True)
    centred = values - average
    variance = jnp.mean(centred * centred, axis=0, keepdims=True)
    normal = (centred * lax.rsqrt(variance + EPSILON)).reshape(128, rows * 128).astype(BF)
    update = lax.dot_general(
        normal, out_weight_ref[...], (((0,), (0,)), ((), ())), preferred_element_type=F32
    )
    out_ref[...] = (state + update * gate).astype(BF).reshape(rows, 128, 128)


def whole(shape):
    return pl.BlockSpec(shape, lambda *_: (0,) * len(shape))


def norm_call(spot, chains, chain_cols, pair, table, bias_weight, rows=16):
    return pl.pallas_call(
        lambda *refs: norm_kernel(*refs, rows=rows),
        grid_spec=pltpu.PrefetchScalarGridSpec(
            num_scalar_prefetch=2,
            grid=(64 // rows,),
            in_specs=[
                whole((8, 128)),
                pl.BlockSpec((rows, 128, 128), lambda g, *_: (g, 0, 0)),
                whole((2 * REACH + 2, 128)),
                whole((HEADS, 128)),
            ],
            out_specs=[
                pl.BlockSpec((rows, 128, 128), lambda g, *_: (g, 0, 0)),
                pl.BlockSpec(
                    (8, 1, HEADS, rows, 128),
                    lambda g, *_: (0, g // (32 // rows), 0, g % (32 // rows), 0),
                ),
            ],
        ),
        out_shape=[
            jax.ShapeDtypeStruct((64, 128, 128), BF),
            jax.ShapeDtypeStruct((8, 2, HEADS, 32, 128), F32),
        ],
        compiler_params=params(),
        cost_estimate=cost(600_000_000, 5_000_000),
        name="pair_norm",
    )(spot, chains, chain_cols, pair, table, bias_weight)


def edge_call(spot, marks, col_mask, normal, weights, rows=16):
    return pl.pallas_call(
        lambda *refs: edge_kernel(*refs, rows=rows),
        grid_spec=pltpu.PrefetchScalarGridSpec(
            num_scalar_prefetch=2,
            grid=(64 // rows,),
            in_specs=[
                whole((8, 128)),
                pl.BlockSpec((rows, 128, 128), lambda g, *_: (g, 0, 0)),
                whole((512, 128)),
            ],
            out_specs=pl.BlockSpec((128, 2, rows, 128), lambda g, *_: (0, 0, g, 0)),
        ),
        out_shape=jax.ShapeDtypeStruct((128, 2, 64, 128), BF),
        compiler_params=params(),
        cost_estimate=cost(2_000_000_000, 6_500_000, 2_000_000),
        name="edges",
    )(spot, marks, col_mask, normal, weights)


def align_call(alignment, weights):
    count, residues, width = alignment.shape
    return pl.pallas_call(
        align_kernel,
        grid=(count,),
        in_specs=[
            pl.BlockSpec((1, residues, width), lambda s: (s, 0, 0)),
            whole((width, 128)),
        ],
        out_specs=[
            pl.BlockSpec((1, residues, 128), lambda s: (s, 0, 0)),
            pl.BlockSpec((1, 128, residues), lambda s: (s, 0, 0)),
        ],
        out_shape=[
            jax.ShapeDtypeStruct((count, residues, 128), BF),
            jax.ShapeDtypeStruct((count, 128, residues), BF),
        ],
        compiler_params=params(),
        cost_estimate=cost(540_000_000, 8_400_000),
        name="align_project",
    )(alignment, weights)


def attend_call(spot, mixed, turned, key_bias, mine, other, first, count):
    residues = mixed.shape[1]
    return pl.pallas_call(
        attend_kernel,
        grid_spec=pltpu.PrefetchScalarGridSpec(
            num_scalar_prefetch=1,
            grid=(count,),
            in_specs=[
                pl.BlockSpec((1, residues, 128), lambda s, *_: (s + first, 0, 0)),
                pl.BlockSpec((1, 128, residues), lambda s, *_: (s + first, 0, 0)),
                pl.BlockSpec((1, 1, residues), lambda s, *_: (s + first, 0, 0)),
            ]
            + [pl.BlockSpec(memory_space=pl.ANY)] * 2,
            out_specs=pl.BlockSpec((1, HEAD_DIM, residues), lambda s, *_: (s, 0, 0)),
            scratch_shapes=[
                pltpu.VMEM((16, 8, 2, 32, 128), F32),
                pltpu.SemaphoreType.DMA((2,)),
            ],
        ),
        out_shape=jax.ShapeDtypeStruct((count, HEAD_DIM, residues), BF),
        compiler_params=params(),
        cost_estimate=cost(count * 1_500_000_000, 5_000_000, count * 1_000_000),
        name="attend",
    )(spot, mixed, turned, key_bias, mine, other)


def merge_call(heads, alignment, weight, pieces, first, count, before=None):
    _, residues, width = alignment.shape
    extra = [] if before is None else [before]
    return pl.pallas_call(
        merge_kernel,
        grid_spec=pltpu.PrefetchScalarGridSpec(
            num_scalar_prefetch=1,
            grid=(count,),
            in_specs=[
                pl.BlockSpec((1, residues, width), lambda s, *_: (s + first, 0, 0)),
                whole((width, width)),
            ]
            + [
                pl.BlockSpec((1, HEAD_DIM, residues), lambda s, *_, k=k: (s + k, 0, 0))
                for _, k in pieces
            ]
            + [pl.BlockSpec(memory_space=pl.ANY)] * len(extra),
            out_specs=pl.BlockSpec((1, residues, width), lambda s, *_: (s + first, 0, 0)),
        ),
        out_shape=jax.ShapeDtypeStruct(alignment.shape, BF),
        input_output_aliases={3 + HEADS: 0} if extra else {},
        compiler_params=params(),
        cost_estimate=cost(count * 140_000_000, count * 1_600_000),
        name="merge_heads",
    )(heads, alignment, weight, *[piece for piece, _ in pieces], *extra)


def triangle_call(received, groups=8):
    return pl.pallas_call(
        triangle_kernel,
        grid=(16 // groups,),
        in_specs=[
            pl.BlockSpec((groups, 8, 1, 64, 128), lambda g: (g, 0, 0, 0, 0)),
            pl.BlockSpec((16, 8, 1, 64, 128), lambda g: (0, 0, 1, 0, 0)),
        ],
        out_specs=pl.BlockSpec((groups, 8, 64, 128), lambda g: (g, 0, 0, 0)),
        out_shape=jax.ShapeDtypeStruct((16, 8, 64, 128), BF),
        compiler_params=params(),
        cost_estimate=cost(2_147_483_648, 6_300_000),
        name="triangle",
    )(received, received)


def update_call(spot, chains, chain_cols, pair, table, normal, triangle, gate_w, out_w, rows=16):
    return pl.pallas_call(
        lambda *refs: update_kernel(*refs, rows=rows),
        grid_spec=pltpu.PrefetchScalarGridSpec(
            num_scalar_prefetch=2,
            grid=(64 // rows,),
            in_specs=[
                whole((8, 128)),
                pl.BlockSpec((rows, 128, 128), lambda g, *_: (g, 0, 0)),
                whole((2 * REACH + 2, 128)),
                pl.BlockSpec((rows, 128, 128), lambda g, *_: (g, 0, 0)),
                pl.BlockSpec((128, rows, 128), lambda g, *_: (0, g, 0)),
                whole((128, 128)),
                whole((128, 128)),
            ],
            out_specs=pl.BlockSpec((rows, 128, 128), lambda g, *_: (g, 0, 0)),
        ),
        out_shape=jax.ShapeDtypeStruct((64, 128, 128), BF),
        compiler_params=params(),
        cost_estimate=cost(900_000_000, 8_400_000, 1_000_000),
        name="pair_update",
    )(spot, chains, chain_cols, pair, table, normal, triangle, gate_w, out_w)


def on_device(
    alignment,
    align_mask,
    residue_mask,
    chain_index,
    pair_input,
    offset_table,
    bias_weight,
    query_weight,
    key_weight,
    value_weight,
    gate_weight,
    output_weight,
    left_gate_weight,
    left_weight,
    right_gate_weight,
    right_weight,
    update_gate_weight,
    update_out_weight,
):
    dap = lax.axis_index("dap")
    hc = lax.axis_index("hc")
    spot = jnp.stack([dap * 64, hc * 128, dap % 2]).astype(jnp.int32)
    chain_cols = chain_index.reshape(8, 128)
    normal, bias = norm_call(
        spot, chain_index, chain_cols, pair_input, offset_table, bias_weight.T
    )

    mine = lax.all_to_all(
        bias.reshape(128, 32, 128), AXES, split_axis=0, concat_axis=0, tiled=True
    )

    qkvg = jnp.concatenate([query_weight, key_weight, value_weight, gate_weight], axis=1)
    mixed, turned = align_call(alignment, qkvg)
    key_bias = MASKED * ((align_mask * residue_mask[None, :]).astype(F32) - 1.0)
    key_bias = key_bias[:, None, :]
    edge_weights = jnp.concatenate(
        [left_gate_weight.T, left_weight.T, right_gate_weight.T, right_weight.T], axis=0
    )
    edges = edge_call(
        spot, residue_mask, residue_mask.reshape(8, 128), normal, edge_weights
    )
    mine, edges, mixed, turned, key_bias = lax.optimization_barrier(
        (mine, edges, mixed, turned, key_bias)
    )
    other = shift(mine, lambda x, y, z, core: (x, y, z, 1 - core))
    mine = mine.reshape(16, 8, 32, 128)
    other = other.reshape(16, 8, 32, 128)
    received = lax.all_to_all(edges, AXES, split_axis=0, concat_axis=0, tiled=True)

    one = attend_call(spot, mixed, turned, key_bias, mine, other, 0, 4)
    two = attend_call(spot, mixed, turned, key_bias, mine, other, 4, 4)

    over_z = lambda x, y, z, core: (x, y, z ^ 1, core)
    along = [lambda x, y, z, core, d=d: (x + d, y, z, core) for d in (1, 3, 2)]
    one_z, two_z = shift(one, over_z), shift(two, over_z)
    two_x = [shift(two, move) for move in along]
    received = lax.optimization_barrier((received, one, two))[0]
    triangle = triangle_call(received.reshape(16, 8, 2, 64, 128))
    triangle = lax.optimization_barrier((triangle, one_z, two_z, two_x))[0]
    one_both = jnp.concatenate([one, one_z], axis=0)
    one_x = [shift(one_both, move) for move in along]
    two_xz = shift(jnp.concatenate(two_x, axis=0), over_z)
    ones = [(one, 0), (one_z, 0)] + [(one_x[k], 4 * f) for f in (0, 1) for k in range(3)]
    twos = [(two, 0), (two_z, 0)] + [(piece, 0) for piece in two_x]
    spot_x, spot_z = hc // 2, hc % 2
    order = jnp.stack(
        [
            ((spot_x - d) % 4) * 2 + (spot_z ^ f)
            for d, f in ((0, 0), (0, 1), (1, 0), (3, 0), (2, 0), (1, 1), (3, 1), (2, 1))
        ]
    ).astype(jnp.int32)

    back = lax.all_to_all(
        triangle.reshape(128, 64, 128), AXES, split_axis=0, concat_axis=0, tiled=True
    )
    pair_out = update_call(
        spot, chain_index, chain_cols, pair_input, offset_table, normal, back,
        update_gate_weight, update_out_weight
    )
    two_xz, pair_out = lax.optimization_barrier((two_xz, pair_out))
    twos = twos + [(two_xz, 4 * k) for k in range(3)]
    alignment_out = merge_call(order, alignment, output_weight, twos, 4, 4)
    alignment_out = merge_call(
        order, alignment, output_weight, ones, 0, 4, alignment_out
    )
    return (alignment_out, pair_out)


def solution(mesh):
    placed = (
        P("dap", None, None),
        P("dap", None),
        P(),
        P(),
        P("dap", "hc", None),
        P(),
        P(),
        P(None, "hc"),
        P(None, "hc"),
        P(None, "hc"),
        P(None, "hc"),
        P(),
        P(),
        P(),
        P(),
        P(),
        P(),
        P(),
    )
    return jax.shard_map(
        on_device,
        mesh=mesh,
        in_specs=placed,
        out_specs=(P("dap", None, None), P("dap", "hc", None)),
        check_vma=False,
    )
```

```python
import jax
import jax.numpy as jnp
from jax import lax
from jax.experimental import pallas as pl
from jax.experimental.pallas import tpu as pltpu
from jax.sharding import PartitionSpec as P

HEADS = 8
HEAD_DIM = 32
REACH = 32
EPSILON = 1e-05
MASKED = 1000000000.0
AXES = ("dap", "hc")
BF = jnp.bfloat16
F32 = jnp.float32
VMEM_BYTES = 60 * 1024 * 1024


SMALL_BYTES = 28 * 1024 * 1024


def params(size=VMEM_BYTES):
    return pltpu.CompilerParams(vmem_limit_bytes=size)


def cost(flops, moved, transcendentals=0):
    return pl.CostEstimate(
        flops=flops, bytes_accessed=moved, transcendentals=transcendentals
    )


def place(x, y, z, core):
    dap = (y % 4) * 4 + ((z % 4) // 2) * 2 + core
    return dap * 8 + (x % 4) * 2 + z % 2


def shift(array, move):
    pairs = []
    for x in range(4):
        for y in range(4):
            for z in range(4):
                for core in range(2):
                    pairs.append((place(x, y, z, core), place(*move(x, y, z, core))))
    return lax.ppermute(array, AXES, pairs)


def over_lanes(values):
    average = jnp.mean(values, axis=-1, keepdims=True)
    centred = values - average
    variance = jnp.mean(centred * centred, axis=-1, keepdims=True)
    return centred * lax.rsqrt(variance + EPSILON)


def pair_states(spot, chains_smem, chains_ref, pair_ref, table_ref, rows, first):
    cols = 128
    slots = table_ref.shape[0]
    chain_row = chains_ref[pl.ds(spot[1] // cols, 1), :].astype(F32)
    chain_rows = jnp.broadcast_to(chain_row, (cols, cols)).T[:, :slots].astype(jnp.int32)
    column = lax.broadcasted_iota(jnp.int32, (cols, slots), 0) + spot[1]
    lane = lax.broadcasted_iota(jnp.int32, (cols, slots), 1)
    parts = []
    for r in range(rows):
        row = spot[0] + first + r
        offset = jnp.clip(row - column + REACH, 0, 2 * REACH)
        slot = jnp.where(chain_rows == chains_smem[row], offset, 2 * REACH + 1)
        parts.append((slot == lane).astype(F32).astype(BF))
    one_hot = jnp.concatenate(parts, axis=0)
    encoded = jnp.dot(one_hot, table_ref[...], preferred_element_type=F32)
    return pair_ref[...].reshape(rows * cols, 128).astype(F32) + encoded


def norm_kernel(
    spot, chains, chain_rows_ref, pair_ref, table_ref, bias_weight_ref, bias_ref, rows
):
    step = pl.program_id(0)
    state = pair_states(
        spot, chains, chain_rows_ref, pair_ref, table_ref, rows, step * rows
    )
    normal = over_lanes(state).astype(BF)
    bias = lax.dot_general(
        bias_weight_ref[...], normal, (((1,), (1,)), ((), ())), preferred_element_type=F32
    )
    bias_ref[...] = jnp.broadcast_to(bias.reshape(1, 1, HEADS, rows, 128), bias_ref.shape)


def edge_kernel(
    spot, chains, marks, chain_rows_ref, pair_ref, table_ref, col_mask_ref, weight_ref, norm_ref,
    out_ref, rows
):
    step = pl.program_id(0)
    state = pair_states(
        spot, chains, chain_rows_ref, pair_ref, table_ref, rows, step * rows
    )
    normal = over_lanes(state).astype(BF)
    norm_ref[...] = normal.reshape(rows, 128, 128)
    col_mask = col_mask_ref[pl.ds(spot[1] // 128, 1), :].astype(F32)
    mask_row = jnp.concatenate(
        [
            col_mask * marks[spot[0] + step * rows + r].astype(F32)
            for r in range(rows)
        ],
        axis=1,
    )
    for side in range(2):
        both = lax.dot_general(
            weight_ref[side * 256 : side * 256 + 256, :],
            normal,
            (((1,), (1,)), ((), ())),
            preferred_element_type=F32,
        )
        edge = jax.nn.sigmoid(both[:128]) * both[128:] * mask_row
        out_ref[:, side] = edge.astype(BF).reshape(128, rows, 128)


def align_kernel(align_ref, weight_ref, out_ref, turned_ref):
    normal = over_lanes(align_ref[0].astype(F32)).astype(BF)
    both = jnp.dot(normal, weight_ref[...], preferred_element_type=F32)
    lane = lax.broadcasted_iota(jnp.int32, both.shape, 1)
    both = jnp.where(lane < HEAD_DIM, both * (HEAD_DIM ** (-0.5)), both)
    out_ref[0] = both.astype(BF)
    turned_ref[0] = both.T.astype(BF)


def attend_kernel(spot, mixed_ref, turned_ref, key_bias_ref, mine_ref, other_ref, out_ref, bias, sems):
    @pl.when(pl.program_id(0) == 0)
    def _():
        one = pltpu.make_async_copy(mine_ref, bias.at[:, :, spot[2]], sems.at[0])
        two = pltpu.make_async_copy(other_ref, bias.at[:, :, 1 - spot[2]], sems.at[1])
        one.start()
        two.start()
        one.wait()
        two.wait()

    keys = turned_ref[0, HEAD_DIM : 2 * HEAD_DIM, :]
    width = mixed_ref.shape[1]
    lane = lax.broadcasted_iota(jnp.int32, (width, 2 * HEAD_DIM), 1)
    values = mixed_ref[0][:, 2 * HEAD_DIM :]
    values = jnp.where(lane < HEAD_DIM, values, jnp.ones_like(values))
    masking = key_bias_ref[0]
    blocks = 4
    rows = blocks * 64
    count = width // rows

    def scores_of(r):
        return jnp.dot(
            mixed_ref[0, r * rows : (r + 1) * rows, :HEAD_DIM], keys, preferred_element_type=F32
        )

    def weights_of(r, scores):
        added = jnp.concatenate(
            [
                bias[r * blocks : (r + 1) * blocks, h].reshape(rows, 128)
                for h in range(HEADS)
            ],
            axis=1,
        )
        scores = scores + added + masking
        return jnp.exp(scores - jnp.max(scores, axis=1, keepdims=True)).astype(BF)

    def finish(r, weights):
        here = slice(r * rows, (r + 1) * rows)
        total = jnp.dot(weights, values, preferred_element_type=F32).T
        gates = turned_ref[0, 3 * HEAD_DIM :, here].astype(F32)
        result = total[:HEAD_DIM] / total[HEAD_DIM:] * jax.nn.sigmoid(gates)
        out_ref[0, :, here] = result.astype(BF)

    scores, weights = scores_of(0), None
    for r in range(count):
        coming = scores_of(r + 1) if r + 1 < count else None
        raised = weights_of(r, scores)
        if r > 0:
            finish(r - 1, weights)
        scores, weights = coming, raised
    finish(count - 1, weights)


def merge_kernel(heads, align_ref, weight_ref, *refs):
    out_ref = refs[-1]
    pieces = refs[: HEADS]
    weight = jnp.concatenate(
        [
            weight_ref[pl.ds(pl.multiple_of(heads[p] * HEAD_DIM, HEAD_DIM), HEAD_DIM), :]
            for p in range(HEADS)
        ],
        axis=0,
    )
    for k in range(out_ref.shape[0]):
        merged = jnp.concatenate([piece[k] for piece in pieces], axis=0)
        update = lax.dot_general(
            merged, weight, (((0,), (0,)), ((), ())), preferred_element_type=F32
        )
        out_ref[k] = (align_ref[k].astype(F32) + update).astype(BF)


def triangle_kernel(left_ref, right_ref, out_ref):
    groups = left_ref.shape[0]
    rows = groups * 64
    residues = right_ref.shape[0] * 64
    total = jnp.zeros((rows, residues), F32)
    for h in range(0, 8, 2):
        left = jnp.concatenate(
            [left_ref[:, h + k, 0].reshape(rows, 128) for k in range(2)], axis=1
        )
        right = jnp.concatenate(
            [right_ref[:, h + k, 0].reshape(residues, 128) for k in range(2)], axis=1
        )
        total = total + lax.dot_general(
            left, right, (((1,), (1,)), ((), ())), preferred_element_type=F32
        )
    for h in range(8):
        out_ref[:, h] = total[:, h * 128 : h * 128 + 128].astype(BF).reshape(groups, 64, 128)


def update_kernel(
    spot, chains, chain_rows_ref, pair_ref, table_ref, norm_ref, triangle_ref, gate_weight_ref,
    out_weight_ref, out_ref, rows
):
    step = pl.program_id(0)
    state = pair_states(
        spot, chains, chain_rows_ref, pair_ref, table_ref, rows, step * rows
    )
    gate = jax.nn.sigmoid(
        jnp.dot(
            norm_ref[...].reshape(rows * 128, 128),
            gate_weight_ref[...],
            preferred_element_type=F32,
        )
    )
    values = triangle_ref[...].astype(F32)
    average = jnp.mean(values, axis=0, keepdims=True)
    centred = values - average
    variance = jnp.mean(centred * centred, axis=0, keepdims=True)
    normal = (centred * lax.rsqrt(variance + EPSILON)).reshape(128, rows * 128).astype(BF)
    update = lax.dot_general(
        normal, out_weight_ref[...], (((0,), (0,)), ((), ())), preferred_element_type=F32
    )
    out_ref[...] = (state + update * gate).astype(BF).reshape(rows, 128, 128)


def whole(shape):
    return pl.BlockSpec(shape, lambda *_: (0,) * len(shape))


def norm_call(spot, chains, chain_rows, pair, table, bias_weight, rows=16):
    return pl.pallas_call(
        lambda *refs: norm_kernel(*refs, rows=rows),
        grid_spec=pltpu.PrefetchScalarGridSpec(
            num_scalar_prefetch=2,
            grid=(64 // rows,),
            in_specs=[
                whole((8, 128)),
                pl.BlockSpec((rows, 128, 128), lambda g, *_: (g, 0, 0)),
                whole((2 * REACH + 2, 128)),
                whole((HEADS, 128)),
            ],
            out_specs=pl.BlockSpec(
                (8, 1, HEADS, rows, 128),
                lambda g, *_: (0, g // (32 // rows), 0, g % (32 // rows), 0),
            ),
        ),
        out_shape=jax.ShapeDtypeStruct((8, 2, HEADS, 32, 128), F32),
        compiler_params=params(),
        cost_estimate=cost(600_000_000, 5_000_000),
        name="pair_norm",
    )(spot, chains, chain_rows, pair, table, bias_weight)


def edge_call(spot, chains, marks, chain_rows, pair, table, col_mask, weights, rows=16):
    return pl.pallas_call(
        lambda *refs: edge_kernel(*refs, rows=rows),
        grid_spec=pltpu.PrefetchScalarGridSpec(
            num_scalar_prefetch=3,
            grid=(64 // rows,),
            in_specs=[
                whole((8, 128)),
                pl.BlockSpec((rows, 128, 128), lambda g, *_: (g, 0, 0)),
                whole((2 * REACH + 2, 128)),
                whole((8, 128)),
                whole((512, 128)),
            ],
            out_specs=[
                pl.BlockSpec((rows, 128, 128), lambda g, *_: (g, 0, 0)),
                pl.BlockSpec((128, 2, rows, 128), lambda g, *_: (0, 0, g, 0)),
            ],
        ),
        out_shape=[
            jax.ShapeDtypeStruct((64, 128, 128), BF),
            jax.ShapeDtypeStruct((128, 2, 64, 128), BF),
        ],
        compiler_params=params(),
        cost_estimate=cost(2_600_000_000, 8_500_000, 2_000_000),
        name="edges",
    )(spot, chains, marks, chain_rows, pair, table, col_mask, weights)


def align_call(alignment, weights):
    count, residues, width = alignment.shape
    return pl.pallas_call(
        align_kernel,
        grid=(count,),
        in_specs=[
            pl.BlockSpec((1, residues, width), lambda s: (s, 0, 0)),
            whole((width, 128)),
        ],
        out_specs=[
            pl.BlockSpec((1, residues, 128), lambda s: (s, 0, 0)),
            pl.BlockSpec((1, 128, residues), lambda s: (s, 0, 0)),
        ],
        out_shape=[
            jax.ShapeDtypeStruct((count, residues, 128), BF),
            jax.ShapeDtypeStruct((count, 128, residues), BF),
        ],
        compiler_params=params(),
        cost_estimate=cost(540_000_000, 8_400_000),
        name="align_project",
    )(alignment, weights)


def attend_call(spot, mixed, turned, key_bias, mine, other, first, count):
    residues = mixed.shape[1]
    return pl.pallas_call(
        attend_kernel,
        grid_spec=pltpu.PrefetchScalarGridSpec(
            num_scalar_prefetch=1,
            grid=(count,),
            in_specs=[
                pl.BlockSpec((1, residues, 128), lambda s, *_: (s + first, 0, 0)),
                pl.BlockSpec((1, 128, residues), lambda s, *_: (s + first, 0, 0)),
                pl.BlockSpec((1, 1, residues), lambda s, *_: (s + first, 0, 0)),
            ]
            + [pl.BlockSpec(memory_space=pl.ANY)] * 2,
            out_specs=pl.BlockSpec((1, HEAD_DIM, residues), lambda s, *_: (s, 0, 0)),
            scratch_shapes=[
                pltpu.VMEM((16, 8, 2, 32, 128), F32),
                pltpu.SemaphoreType.DMA((2,)),
            ],
        ),
        out_shape=jax.ShapeDtypeStruct((count, HEAD_DIM, residues), BF),
        compiler_params=params(),
        cost_estimate=cost(count * 1_500_000_000, 5_000_000, count * 1_000_000),
        name="attend",
    )(spot, mixed, turned, key_bias, mine, other)


def merge_call(heads, alignment, weight, pieces, first, count, before=None, per=2):
    _, residues, width = alignment.shape
    extra = [] if before is None else [before]
    return pl.pallas_call(
        merge_kernel,
        grid_spec=pltpu.PrefetchScalarGridSpec(
            num_scalar_prefetch=1,
            grid=(count // per,),
            in_specs=[
                pl.BlockSpec((per, residues, width), lambda s, *_: (s + first // per, 0, 0)),
                whole((width, width)),
            ]
            + [
                pl.BlockSpec((per, HEAD_DIM, residues), lambda s, *_, k=k: (s + k // per, 0, 0))
                for _, k in pieces
            ]
            + [pl.BlockSpec(memory_space=pl.ANY)] * len(extra),
            out_specs=pl.BlockSpec((per, residues, width), lambda s, *_: (s + first // per, 0, 0)),
        ),
        out_shape=jax.ShapeDtypeStruct(alignment.shape, BF),
        input_output_aliases={3 + HEADS: 0} if extra else {},
        compiler_params=params(SMALL_BYTES),
        cost_estimate=cost(count * 140_000_000, count * 1_600_000),
        name="merge_heads",
    )(heads, alignment, weight, *[piece for piece, _ in pieces], *extra)


def triangle_call(received, groups=8):
    return pl.pallas_call(
        triangle_kernel,
        grid=(16 // groups,),
        in_specs=[
            pl.BlockSpec((groups, 8, 1, 64, 128), lambda g: (g, 0, 0, 0, 0)),
            pl.BlockSpec((16, 8, 1, 64, 128), lambda g: (0, 0, 1, 0, 0)),
        ],
        out_specs=pl.BlockSpec((groups, 8, 64, 128), lambda g: (g, 0, 0, 0)),
        out_shape=jax.ShapeDtypeStruct((16, 8, 64, 128), BF),
        compiler_params=params(),
        cost_estimate=cost(2_147_483_648, 6_300_000),
        name="triangle",
    )(received, received)


def update_call(spot, chains, chain_rows, pair, table, normal, triangle, gate_w, out_w, rows=16):
    return pl.pallas_call(
        lambda *refs: update_kernel(*refs, rows=rows),
        grid_spec=pltpu.PrefetchScalarGridSpec(
            num_scalar_prefetch=2,
            grid=(64 // rows,),
            in_specs=[
                whole((8, 128)),
                pl.BlockSpec((rows, 128, 128), lambda g, *_: (g, 0, 0)),
                whole((2 * REACH + 2, 128)),
                pl.BlockSpec((rows, 128, 128), lambda g, *_: (g, 0, 0)),
                pl.BlockSpec((128, rows, 128), lambda g, *_: (0, g, 0)),
                whole((128, 128)),
                whole((128, 128)),
            ],
            out_specs=pl.BlockSpec((rows, 128, 128), lambda g, *_: (g, 0, 0)),
        ),
        out_shape=jax.ShapeDtypeStruct((64, 128, 128), BF),
        compiler_params=params(),
        cost_estimate=cost(900_000_000, 8_400_000, 1_000_000),
        name="pair_update",
    )(spot, chains, chain_rows, pair, table, normal, triangle, gate_w, out_w)


def on_device(
    alignment,
    align_mask,
    residue_mask,
    chain_index,
    pair_input,
    offset_table,
    bias_weight,
    query_weight,
    key_weight,
    value_weight,
    gate_weight,
    output_weight,
    left_gate_weight,
    left_weight,
    right_gate_weight,
    right_weight,
    update_gate_weight,
    update_out_weight,
):
    dap = lax.axis_index("dap")
    hc = lax.axis_index("hc")
    spot = jnp.stack([dap * 64, hc * 128, dap % 2]).astype(jnp.int32)
    chain_rows = chain_index.reshape(8, 128)
    bias = norm_call(
        spot, chain_index, chain_rows, pair_input, offset_table, bias_weight.T
    )

    mine = lax.all_to_all(
        bias.reshape(128, 32, 128), AXES, split_axis=0, concat_axis=0, tiled=True
    )

    qkvg = jnp.concatenate([query_weight, key_weight, value_weight, gate_weight], axis=1)
    mixed, turned = align_call(alignment, qkvg)
    key_bias = MASKED * ((align_mask * residue_mask[None, :]).astype(F32) - 1.0)
    key_bias = key_bias[:, None, :]
    edge_weights = jnp.concatenate(
        [left_gate_weight.T, left_weight.T, right_gate_weight.T, right_weight.T], axis=0
    )
    normal, edges = edge_call(
        spot, chain_index, residue_mask, chain_rows, pair_input, offset_table,
        residue_mask.reshape(8, 128), edge_weights
    )
    mine, edges, mixed, turned, key_bias = lax.optimization_barrier(
        (mine, edges, mixed, turned, key_bias)
    )
    other = shift(mine, lambda x, y, z, core: (x, y, z, 1 - core))
    mine = mine.reshape(16, 8, 32, 128)
    other = other.reshape(16, 8, 32, 128)
    received = lax.all_to_all(edges, AXES, split_axis=0, concat_axis=0, tiled=True)

    heads = attend_call(spot, mixed, turned, key_bias, mine, other, 0, 8)

    over_z = lambda x, y, z, core: (x, y, z ^ 1, core)
    along = [lambda x, y, z, core, d=d: (x + d, y, z, core) for d in (1, 3, 2)]
    heads_z = shift(heads, over_z)
    second = heads[4:]
    second_x = [shift(second, move) for move in along]
    received = lax.optimization_barrier((received, heads))[0]
    triangle = triangle_call(received.reshape(16, 8, 2, 64, 128))
    triangle = lax.optimization_barrier((triangle, second_x, heads_z))[0]
    first = jnp.concatenate([heads[:4], heads_z[:4]], axis=0)
    first_x = [shift(first, move) for move in along]
    second_xz = shift(jnp.concatenate(second_x, axis=0), over_z)
    ones = [(heads, 0), (heads_z, 0)]
    ones = ones + [(piece, 4 * f) for f in (0, 1) for piece in first_x]
    twos = [(heads, 4), (heads_z, 4)] + [(piece, 0) for piece in second_x]
    spot_x, spot_z = hc // 2, hc % 2
    order = jnp.stack(
        [
            ((spot_x - d) % 4) * 2 + (spot_z ^ f)
            for d, f in ((0, 0), (0, 1), (1, 0), (3, 0), (2, 0), (1, 1), (3, 1), (2, 1))
        ]
    ).astype(jnp.int32)

    back = lax.all_to_all(
        triangle.reshape(128, 64, 128), AXES, split_axis=0, concat_axis=0, tiled=True
    )
    pair_out = update_call(
        spot, chain_index, chain_rows, pair_input, offset_table, normal, back,
        update_gate_weight, update_out_weight
    )
    second_xz, pair_out = lax.optimization_barrier((second_xz, pair_out))
    twos = twos + [(second_xz, 4 * k) for k in range(3)]
    alignment_out = merge_call(order, alignment, output_weight, twos, 4, 4)
    alignment_out = merge_call(
        order, alignment, output_weight, ones, 0, 4, alignment_out
    )
    return (alignment_out, pair_out)


def solution(mesh):
    placed = (
        P("dap", None, None),
        P("dap", None),
        P(),
        P(),
        P("dap", "hc", None),
        P(),
        P(),
        P(None, "hc"),
        P(None, "hc"),
        P(None, "hc"),
        P(None, "hc"),
        P(),
        P(),
        P(),
        P(),
        P(),
        P(),
        P(),
    )
    return jax.shard_map(
        on_device,
        mesh=mesh,
        in_specs=placed,
        out_specs=(P("dap", None, None), P("dap", "hc", None)),
        check_vma=False,
    )
```

```python
import jax
import jax.numpy as jnp
from jax import lax
from jax.experimental import pallas as pl
from jax.experimental.pallas import tpu as pltpu
from jax.sharding import PartitionSpec as P

HEADS = 8
HEAD_DIM = 32
REACH = 32
EPSILON = 1e-05
MASKED = 1000000000.0
AXES = ("dap", "hc")
BF = jnp.bfloat16
F32 = jnp.float32
VMEM_BYTES = 60 * 1024 * 1024


SMALL_BYTES = 28 * 1024 * 1024


def params(size=VMEM_BYTES):
    return pltpu.CompilerParams(vmem_limit_bytes=size)


def cost(flops, moved, transcendentals=0):
    return pl.CostEstimate(
        flops=flops, bytes_accessed=moved, transcendentals=transcendentals
    )


def place(x, y, z, core):
    dap = (y % 4) * 4 + ((z % 4) // 2) * 2 + core
    return dap * 8 + (x % 4) * 2 + z % 2


def shift(array, move):
    pairs = []
    for x in range(4):
        for y in range(4):
            for z in range(4):
                for core in range(2):
                    pairs.append((place(x, y, z, core), place(*move(x, y, z, core))))
    return lax.ppermute(array, AXES, pairs)


def over_lanes(values):
    average = jnp.mean(values, axis=-1, keepdims=True)
    centred = values - average
    variance = jnp.mean(centred * centred, axis=-1, keepdims=True)
    return centred * lax.rsqrt(variance + EPSILON)


def pair_states(spot, chains_smem, chains_ref, pair_ref, table_ref, rows, first):
    cols = 128
    slots = table_ref.shape[0]
    chain_row = chains_ref[pl.ds(spot[1] // cols, 1), :].astype(F32)
    chain_rows = jnp.broadcast_to(chain_row, (cols, cols)).T[:, :slots].astype(jnp.int32)
    column = lax.broadcasted_iota(jnp.int32, (cols, slots), 0) + spot[1]
    lane = lax.broadcasted_iota(jnp.int32, (cols, slots), 1)
    parts = []
    for r in range(rows):
        row = spot[0] + first + r
        offset = jnp.clip(row - column + REACH, 0, 2 * REACH)
        slot = jnp.where(chain_rows == chains_smem[row], offset, 2 * REACH + 1)
        parts.append((slot == lane).astype(F32).astype(BF))
    one_hot = jnp.concatenate(parts, axis=0)
    encoded = jnp.dot(one_hot, table_ref[...], preferred_element_type=F32)
    return pair_ref[...].reshape(rows * cols, 128).astype(F32) + encoded


def norm_kernel(
    row_first, col_first, chains, chain_rows_ref, pair_ref, table_ref, bias_weight_ref, bias_ref, rows
):
    step = pl.program_id(0)
    spot = (row_first[0], col_first[0])
    state = pair_states(
        spot, chains, chain_rows_ref, pair_ref, table_ref, rows, step * rows
    )
    normal = over_lanes(state).astype(BF)
    bias = lax.dot_general(
        bias_weight_ref[...], normal, (((1,), (1,)), ((), ())), preferred_element_type=F32
    )
    bias_ref[...] = jnp.broadcast_to(bias.reshape(1, 1, HEADS, rows, 128), bias_ref.shape)


def edge_kernel(
    spot, chains, marks, chain_rows_ref, pair_ref, table_ref, col_mask_ref, weight_ref, norm_ref,
    out_ref, rows
):
    step = pl.program_id(0)
    state = pair_states(
        spot, chains, chain_rows_ref, pair_ref, table_ref, rows, step * rows
    )
    normal = over_lanes(state).astype(BF)
    norm_ref[...] = normal.reshape(rows, 128, 128)
    col_mask = col_mask_ref[pl.ds(spot[1] // 128, 1), :].astype(F32)
    mask_row = jnp.concatenate(
        [
            col_mask * marks[spot[0] + step * rows + r].astype(F32)
            for r in range(rows)
        ],
        axis=1,
    )
    for side in range(2):
        both = lax.dot_general(
            weight_ref[side * 256 : side * 256 + 256, :],
            normal,
            (((1,), (1,)), ((), ())),
            preferred_element_type=F32,
        )
        edge = jax.nn.sigmoid(both[:128]) * both[128:] * mask_row
        out_ref[:, side] = edge.astype(BF).reshape(128, rows, 128)


def align_kernel(align_ref, weight_ref, out_ref, turned_ref):
    normal = over_lanes(align_ref[0].astype(F32)).astype(BF)
    both = jnp.dot(normal, weight_ref[...], preferred_element_type=F32)
    lane = lax.broadcasted_iota(jnp.int32, both.shape, 1)
    both = jnp.where(lane < HEAD_DIM, both * (HEAD_DIM ** (-0.5)), both)
    out_ref[0] = both.astype(BF)
    turned_ref[0] = both.T.astype(BF)


def attend_kernel(spot, mixed_ref, turned_ref, key_bias_ref, mine_ref, other_ref, out_ref, bias, sems):
    @pl.when(pl.program_id(0) == 0)
    def _():
        one = pltpu.make_async_copy(mine_ref, bias.at[:, :, spot[2]], sems.at[0])
        two = pltpu.make_async_copy(other_ref, bias.at[:, :, 1 - spot[2]], sems.at[1])
        one.start()
        two.start()
        one.wait()
        two.wait()

    keys = turned_ref[0, HEAD_DIM : 2 * HEAD_DIM, :]
    width = mixed_ref.shape[1]
    lane = lax.broadcasted_iota(jnp.int32, (width, 2 * HEAD_DIM), 1)
    values = mixed_ref[0][:, 2 * HEAD_DIM :]
    values = jnp.where(lane < HEAD_DIM, values, jnp.ones_like(values))
    masking = key_bias_ref[0]
    blocks = 4
    rows = blocks * 64
    count = width // rows

    def scores_of(r):
        return jnp.dot(
            mixed_ref[0, r * rows : (r + 1) * rows, :HEAD_DIM], keys, preferred_element_type=F32
        )

    def weights_of(r, scores):
        added = jnp.concatenate(
            [
                bias[r * blocks : (r + 1) * blocks, h].reshape(rows, 128)
                for h in range(HEADS)
            ],
            axis=1,
        )
        scores = scores + added + masking
        return jnp.exp(scores - jnp.max(scores, axis=1, keepdims=True)).astype(BF)

    def finish(r, weights):
        here = slice(r * rows, (r + 1) * rows)
        total = jnp.dot(weights, values, preferred_element_type=F32).T
        gates = turned_ref[0, 3 * HEAD_DIM :, here].astype(F32)
        result = total[:HEAD_DIM] / total[HEAD_DIM:] * jax.nn.sigmoid(gates)
        out_ref[0, :, here] = result.astype(BF)

    scores, weights = scores_of(0), None
    for r in range(count):
        coming = scores_of(r + 1) if r + 1 < count else None
        raised = weights_of(r, scores)
        if r > 0:
            finish(r - 1, weights)
        scores, weights = coming, raised
    finish(count - 1, weights)


def merge_kernel(heads, align_ref, weight_ref, *refs):
    out_ref = refs[-1]
    pieces = refs[: HEADS]
    weight = jnp.concatenate(
        [
            weight_ref[pl.ds(pl.multiple_of(heads[p] * HEAD_DIM, HEAD_DIM), HEAD_DIM), :]
            for p in range(HEADS)
        ],
        axis=0,
    )
    for k in range(out_ref.shape[0]):
        merged = jnp.concatenate([piece[k] for piece in pieces], axis=0)
        update = lax.dot_general(
            merged, weight, (((0,), (0,)), ((), ())), preferred_element_type=F32
        )
        out_ref[k] = (align_ref[k].astype(F32) + update).astype(BF)


def triangle_kernel(left_ref, right_ref, out_ref):
    groups = left_ref.shape[0]
    rows = groups * 64
    residues = right_ref.shape[0] * 64
    total = jnp.zeros((rows, residues), F32)
    for h in range(0, 8, 2):
        left = jnp.concatenate(
            [left_ref[:, h + k, 0].reshape(rows, 128) for k in range(2)], axis=1
        )
        right = jnp.concatenate(
            [right_ref[:, h + k, 0].reshape(residues, 128) for k in range(2)], axis=1
        )
        total = total + lax.dot_general(
            left, right, (((1,), (1,)), ((), ())), preferred_element_type=F32
        )
    for h in range(8):
        out_ref[:, h] = total[:, h * 128 : h * 128 + 128].astype(BF).reshape(groups, 64, 128)


def update_kernel(
    spot, chains, chain_rows_ref, pair_ref, table_ref, norm_ref, triangle_ref, gate_weight_ref,
    out_weight_ref, out_ref, rows
):
    step = pl.program_id(0)
    state = pair_states(
        spot, chains, chain_rows_ref, pair_ref, table_ref, rows, step * rows
    )
    gate = jax.nn.sigmoid(
        jnp.dot(
            norm_ref[...].reshape(rows * 128, 128),
            gate_weight_ref[...],
            preferred_element_type=F32,
        )
    )
    values = triangle_ref[...].astype(F32)
    average = jnp.mean(values, axis=0, keepdims=True)
    centred = values - average
    variance = jnp.mean(centred * centred, axis=0, keepdims=True)
    normal = (centred * lax.rsqrt(variance + EPSILON)).reshape(128, rows * 128).astype(BF)
    update = lax.dot_general(
        normal, out_weight_ref[...], (((0,), (0,)), ((), ())), preferred_element_type=F32
    )
    out_ref[...] = (state + update * gate).astype(BF).reshape(rows, 128, 128)


def whole(shape):
    return pl.BlockSpec(shape, lambda *_: (0,) * len(shape))


def norm_call(row_first, col_first, chains, chain_rows, pair, table, bias_weight, rows=16):
    return pl.pallas_call(
        lambda *refs: norm_kernel(*refs, rows=rows),
        grid_spec=pltpu.PrefetchScalarGridSpec(
            num_scalar_prefetch=3,
            grid=(64 // rows,),
            in_specs=[
                whole((8, 128)),
                pl.BlockSpec((rows, 128, 128), lambda g, *_: (g, 0, 0)),
                whole((2 * REACH + 2, 128)),
                whole((HEADS, 128)),
            ],
            out_specs=pl.BlockSpec(
                (8, 1, HEADS, rows, 128),
                lambda g, *_: (0, g // (32 // rows), 0, g % (32 // rows), 0),
            ),
        ),
        out_shape=jax.ShapeDtypeStruct((8, 2, HEADS, 32, 128), F32),
        compiler_params=params(),
        cost_estimate=cost(600_000_000, 5_000_000),
        name="pair_norm",
    )(row_first, col_first, chains, chain_rows, pair, table, bias_weight)


def edge_call(spot, chains, marks, chain_rows, pair, table, col_mask, weights, rows=16):
    return pl.pallas_call(
        lambda *refs: edge_kernel(*refs, rows=rows),
        grid_spec=pltpu.PrefetchScalarGridSpec(
            num_scalar_prefetch=3,
            grid=(64 // rows,),
            in_specs=[
                whole((8, 128)),
                pl.BlockSpec((rows, 128, 128), lambda g, *_: (g, 0, 0)),
                whole((2 * REACH + 2, 128)),
                whole((8, 128)),
                whole((512, 128)),
            ],
            out_specs=[
                pl.BlockSpec((rows, 128, 128), lambda g, *_: (g, 0, 0)),
                pl.BlockSpec((128, 2, rows, 128), lambda g, *_: (0, 0, g, 0)),
            ],
        ),
        out_shape=[
            jax.ShapeDtypeStruct((64, 128, 128), BF),
            jax.ShapeDtypeStruct((128, 2, 64, 128), BF),
        ],
        compiler_params=params(),
        cost_estimate=cost(2_600_000_000, 8_500_000, 2_000_000),
        name="edges",
    )(spot, chains, marks, chain_rows, pair, table, col_mask, weights)


def align_call(alignment, weights):
    count, residues, width = alignment.shape
    return pl.pallas_call(
        align_kernel,
        grid=(count,),
        in_specs=[
            pl.BlockSpec((1, residues, width), lambda s: (s, 0, 0)),
            whole((width, 128)),
        ],
        out_specs=[
            pl.BlockSpec((1, residues, 128), lambda s: (s, 0, 0)),
            pl.BlockSpec((1, 128, residues), lambda s: (s, 0, 0)),
        ],
        out_shape=[
            jax.ShapeDtypeStruct((count, residues, 128), BF),
            jax.ShapeDtypeStruct((count, 128, residues), BF),
        ],
        compiler_params=params(),
        cost_estimate=cost(540_000_000, 8_400_000),
        name="align_project",
    )(alignment, weights)


def attend_call(spot, mixed, turned, key_bias, mine, other, first, count):
    residues = mixed.shape[1]
    return pl.pallas_call(
        attend_kernel,
        grid_spec=pltpu.PrefetchScalarGridSpec(
            num_scalar_prefetch=1,
            grid=(count,),
            in_specs=[
                pl.BlockSpec((1, residues, 128), lambda s, *_: (s + first, 0, 0)),
                pl.BlockSpec((1, 128, residues), lambda s, *_: (s + first, 0, 0)),
                pl.BlockSpec((1, 1, residues), lambda s, *_: (s + first, 0, 0)),
            ]
            + [pl.BlockSpec(memory_space=pl.ANY)] * 2,
            out_specs=pl.BlockSpec((1, HEAD_DIM, residues), lambda s, *_: (s, 0, 0)),
            scratch_shapes=[
                pltpu.VMEM((16, 8, 2, 32, 128), F32),
                pltpu.SemaphoreType.DMA((2,)),
            ],
        ),
        out_shape=jax.ShapeDtypeStruct((count, HEAD_DIM, residues), BF),
        compiler_params=params(),
        cost_estimate=cost(count * 1_500_000_000, 5_000_000, count * 1_000_000),
        name="attend",
    )(spot, mixed, turned, key_bias, mine, other)


def merge_call(heads, alignment, weight, pieces, first, count, before=None, per=2):
    _, residues, width = alignment.shape
    extra = [] if before is None else [before]
    return pl.pallas_call(
        merge_kernel,
        grid_spec=pltpu.PrefetchScalarGridSpec(
            num_scalar_prefetch=1,
            grid=(count // per,),
            in_specs=[
                pl.BlockSpec((per, residues, width), lambda s, *_: (s + first // per, 0, 0)),
                whole((width, width)),
            ]
            + [
                pl.BlockSpec((per, HEAD_DIM, residues), lambda s, *_, k=k: (s + k // per, 0, 0))
                for _, k in pieces
            ]
            + [pl.BlockSpec(memory_space=pl.ANY)] * len(extra),
            out_specs=pl.BlockSpec((per, residues, width), lambda s, *_: (s + first // per, 0, 0)),
        ),
        out_shape=jax.ShapeDtypeStruct(alignment.shape, BF),
        input_output_aliases={3 + HEADS: 0} if extra else {},
        compiler_params=params(SMALL_BYTES),
        cost_estimate=cost(count * 140_000_000, count * 1_600_000),
        name="merge_heads",
    )(heads, alignment, weight, *[piece for piece, _ in pieces], *extra)


def triangle_call(received, groups=8):
    return pl.pallas_call(
        triangle_kernel,
        grid=(16 // groups,),
        in_specs=[
            pl.BlockSpec((groups, 8, 1, 64, 128), lambda g: (g, 0, 0, 0, 0)),
            pl.BlockSpec((16, 8, 1, 64, 128), lambda g: (0, 0, 1, 0, 0)),
        ],
        out_specs=pl.BlockSpec((groups, 8, 64, 128), lambda g: (g, 0, 0, 0)),
        out_shape=jax.ShapeDtypeStruct((16, 8, 64, 128), BF),
        compiler_params=params(),
        cost_estimate=cost(2_147_483_648, 6_300_000),
        name="triangle",
    )(received, received)


def update_call(spot, chains, chain_rows, pair, table, normal, triangle, gate_w, out_w, rows=16):
    return pl.pallas_call(
        lambda *refs: update_kernel(*refs, rows=rows),
        grid_spec=pltpu.PrefetchScalarGridSpec(
            num_scalar_prefetch=2,
            grid=(64 // rows,),
            in_specs=[
                whole((8, 128)),
                pl.BlockSpec((rows, 128, 128), lambda g, *_: (g, 0, 0)),
                whole((2 * REACH + 2, 128)),
                pl.BlockSpec((rows, 128, 128), lambda g, *_: (g, 0, 0)),
                pl.BlockSpec((128, rows, 128), lambda g, *_: (0, g, 0)),
                whole((128, 128)),
                whole((128, 128)),
            ],
            out_specs=pl.BlockSpec((rows, 128, 128), lambda g, *_: (g, 0, 0)),
        ),
        out_shape=jax.ShapeDtypeStruct((64, 128, 128), BF),
        compiler_params=params(),
        cost_estimate=cost(900_000_000, 8_400_000, 1_000_000),
        name="pair_update",
    )(spot, chains, chain_rows, pair, table, normal, triangle, gate_w, out_w)


def on_device(
    alignment,
    align_mask,
    residue_mask,
    chain_index,
    pair_input,
    offset_table,
    bias_weight,
    query_weight,
    key_weight,
    value_weight,
    gate_weight,
    output_weight,
    left_gate_weight,
    left_weight,
    right_gate_weight,
    right_weight,
    update_gate_weight,
    update_out_weight,
):
    dap = lax.axis_index("dap")
    hc = lax.axis_index("hc")
    spot = jnp.stack([dap * 64, hc * 128, dap % 2]).astype(jnp.int32)
    chain_rows = chain_index.reshape(8, 128)
    bias = norm_call(
        (dap * 64).astype(jnp.int32).reshape(1), (hc * 128).astype(jnp.int32).reshape(1), chain_index, chain_rows, pair_input, offset_table, bias_weight.T
    )

    mine = lax.all_to_all(
        bias.reshape(128, 32, 128), AXES, split_axis=0, concat_axis=0, tiled=True
    )

    qkvg = jnp.concatenate([query_weight, key_weight, value_weight, gate_weight], axis=1)
    mixed, turned = align_call(alignment, qkvg)
    key_bias = MASKED * ((align_mask * residue_mask[None, :]).astype(F32) - 1.0)
    key_bias = key_bias[:, None, :]
    edge_weights = jnp.concatenate(
        [left_gate_weight.T, left_weight.T, right_gate_weight.T, right_weight.T], axis=0
    )
    normal, edges = edge_call(
        spot, chain_index, residue_mask, chain_rows, pair_input, offset_table,
        residue_mask.reshape(8, 128), edge_weights
    )
    mine, edges, mixed, turned, key_bias = lax.optimization_barrier(
        (mine, edges, mixed, turned, key_bias)
    )
    other = shift(mine, lambda x, y, z, core: (x, y, z, 1 - core))
    mine = mine.reshape(16, 8, 32, 128)
    other = other.reshape(16, 8, 32, 128)
    received = lax.all_to_all(edges, AXES, split_axis=0, concat_axis=0, tiled=True)

    heads = attend_call(spot, mixed, turned, key_bias, mine, other, 0, 8)

    over_z = lambda x, y, z, core: (x, y, z ^ 1, core)
    along = [lambda x, y, z, core, d=d: (x + d, y, z, core) for d in (1, 3, 2)]
    heads_z = shift(heads, over_z)
    second = heads[4:]
    second_x = [shift(second, move) for move in along]
    received = lax.optimization_barrier((received, heads))[0]
    triangle = triangle_call(received.reshape(16, 8, 2, 64, 128))
    triangle = lax.optimization_barrier((triangle, second_x, heads_z))[0]
    first = jnp.concatenate([heads[:4], heads_z[:4]], axis=0)
    first_x = [shift(first, move) for move in along]
    second_xz = shift(jnp.concatenate(second_x, axis=0), over_z)
    ones = [(heads, 0), (heads_z, 0)]
    ones = ones + [(piece, 4 * f) for f in (0, 1) for piece in first_x]
    twos = [(heads, 4), (heads_z, 4)] + [(piece, 0) for piece in second_x]
    spot_x, spot_z = hc // 2, hc % 2
    order = jnp.stack(
        [
            ((spot_x - d) % 4) * 2 + (spot_z ^ f)
            for d, f in ((0, 0), (0, 1), (1, 0), (3, 0), (2, 0), (1, 1), (3, 1), (2, 1))
        ]
    ).astype(jnp.int32)

    back = lax.all_to_all(
        triangle.reshape(128, 64, 128), AXES, split_axis=0, concat_axis=0, tiled=True
    )
    pair_out = update_call(
        spot, chain_index, chain_rows, pair_input, offset_table, normal, back,
        update_gate_weight, update_out_weight
    )
    second_xz, pair_out = lax.optimization_barrier((second_xz, pair_out))
    twos = twos + [(second_xz, 4 * k) for k in range(3)]
    alignment_out = merge_call(order, alignment, output_weight, twos, 4, 4)
    alignment_out = merge_call(
        order, alignment, output_weight, ones, 0, 4, alignment_out
    )
    return (alignment_out, pair_out)


def solution(mesh):
    placed = (
        P("dap", None, None),
        P("dap", None),
        P(),
        P(),
        P("dap", "hc", None),
        P(),
        P(),
        P(None, "hc"),
        P(None, "hc"),
        P(None, "hc"),
        P(None, "hc"),
        P(),
        P(),
        P(),
        P(),
        P(),
        P(),
        P(),
    )
    return jax.shard_map(
        on_device,
        mesh=mesh,
        in_specs=placed,
        out_specs=(P("dap", None, None), P("dap", "hc", None)),
        check_vma=False,
    )
```
